32 devices in a mesh: alpha: 16 (over z, y, x), beta: 2 (over core).
Axes of the slice: x: 2, y: 2, z: 4, core: 2. Of those that a mesh axis runs over, the one named last changes fastest.
Arguments:
- coeffs: bfloat16 [128, 2, 256], P('alpha', None, 'beta'), may hold values from -6 to 6
- integrals: bfloat16 [484, 484], replicated, may hold values from -0.03125 to 0.03125
- beta_source: int32 [484, 256], P(None, 'beta'), may hold values from 0 to 255
- beta_sign: int32 [484, 256], P(None, 'beta'), may hold values from -1 to 1
- alpha_slots: int32 [16, 16, 4, 128], P('alpha'), may hold values from -1 to 483, as said below
Outputs:
- sigma: float32 [128, 2, 256], P('alpha', None, 'beta')
The draws below stay inside these ranges and needn't reach their ends.
Inputs may be any that keep to these rules, and one draw needn't show every extreme that they name: alpha_slots[s, d, 0, q], [s, d, 1, q], [s, d, 2, q], [s, d, 3, q] are the source string within block s (below 8), the orbital pair (below 484), the target string within block d (below 8) and the sign (-1 or 1; 0 marks an empty slot, whose other entries mean nothing); in every draw some target block has all 128 slots live from every source block.
All inputs are finite; a program needn't handle non-finite values.
Results may differ from the reference program's by a relative error of at most 0.0029.
Values may be sent and summed in bfloat16 or wider, within the bound.
A program may use at most 64 MiB of HBM per device.

```python
import jax
import jax.numpy as jnp
from jax import lax

P_SIZE = 484
A_DEV = 8
CAP = 128
ABLOCKS = 16
NA = 128
NB = 256


def draw_alpha_slots(key, part):
    shape = (ABLOCKS, ABLOCKS, CAP)
    source_ids = jax.random.randint(jax.random.fold_in(key, 11), shape, 0, A_DEV)
    pair_ids = jax.random.randint(jax.random.fold_in(key, 12), shape, 0, P_SIZE)
    target_ids = jax.random.randint(jax.random.fold_in(key, 13), shape, 0, A_DEV)
    sign_vals = jax.random.randint(jax.random.fold_in(key, 14), shape, 0, 2) * 2 - 1
    hot_rows = jax.random.randint(jax.random.fold_in(key, 15), (ABLOCKS,), 0, 2)
    forced = jax.random.randint(jax.random.fold_in(key, 16), (), 0, ABLOCKS)
    hot_rows = jnp.where(jnp.arange(ABLOCKS) == forced, 1, hot_rows)
    base_count = jax.random.randint(jax.random.fold_in(key, 17), (ABLOCKS, ABLOCKS), CAP // 4, CAP // 2 + 1)
    counts = jnp.where(hot_rows[None, :] == 1, CAP, base_count)
    mult = jax.random.randint(jax.random.fold_in(key, 18), (ABLOCKS, ABLOCKS), 0, CAP // 2) * 2 + 1
    offset = jax.random.randint(jax.random.fold_in(key, 19), (ABLOCKS, ABLOCKS), 0, CAP)
    position = (jnp.arange(CAP)[None, None, :] * mult[:, :, None] + offset[:, :, None]) % CAP
    live = position < counts[:, :, None]
    sign_vals = jnp.where(live, sign_vals, 0)
    return jnp.stack([source_ids, pair_ids, target_ids, sign_vals], axis=2).astype(jnp.int32)


def plant(entries, rng, smallest, largest):
    place = [jax.random.randint(jax.random.fold_in(rng, axis), (), 0, length) for axis, length in enumerate(entries.shape)]
    main_axis = entries.shape.index(max(entries.shape))
    next_to = place[:main_axis] + [(place[main_axis] + 1) % entries.shape[main_axis]] + place[main_axis + 1:]
    return entries.at[tuple(place)].set(smallest).at[tuple(next_to)].set(largest)


def block_scale(own_key, dims, pieces, smallest, high):
    loudness = 1.0
    for dim, blocks in pieces:
        steps = jax.random.uniform(jax.random.fold_in(jax.random.fold_in(own_key, 6), dim), (blocks,), jnp.float32, smallest / len(pieces), high / len(pieces))
        loudness = loudness * jnp.repeat(jnp.exp(steps), dims[dim] // blocks).reshape((-1,) + (1,) * (len(dims) - 1 - dim))
    return loudness


def normal_values(own_key, dims, spread, bound, cuts=(), held_as=jnp.bfloat16):
    loudness = block_scale(own_key, dims, cuts, -0.22, 0.18) if cuts else 1.0
    entries = jax.random.normal(own_key, dims, jnp.float32) * spread * loudness
    return jnp.minimum(jnp.maximum(entries, -bound), bound).astype(held_as)


def setup_inputs(seed: int = 0) -> dict:
    key_list = jax.random.split(jax.random.key(seed), 6)
    coeffs = normal_values(key_list[0], (NA, 2, NB), 1.0, 6.0, ((0, 16), (2, 2)))
    integrals = normal_values(key_list[1], (P_SIZE, P_SIZE), (64 * P_SIZE) ** -0.5, 0.03125)
    beta_source = plant(jax.random.randint(key_list[2], (P_SIZE, NB), 0, NB), jax.random.fold_in(key_list[2], 1), 0, NB - 1).astype(jnp.int32)
    beta_sign = plant(jax.random.randint(key_list[3], (P_SIZE, NB), -1, 2), jax.random.fold_in(key_list[3], 1), -1, 1).astype(jnp.int32)
    alpha_slots = draw_alpha_slots(jax.random.fold_in(key_list[5], 71), 0)
    return {"coeffs": coeffs, "integrals": integrals, "beta_source": beta_source, "beta_sign": beta_sign, "alpha_slots": alpha_slots}


def reference(coeffs, integrals, beta_source, beta_sign, alpha_slots):
    signs_beta = beta_sign.astype(jnp.float32)
    int_mat = integrals.astype(jnp.float32)
    strings = jnp.arange(A_DEV, dtype=jnp.int32)

    def one_block(carry, block_id):
        block_rows = lax.dynamic_slice_in_dim(coeffs, (block_id * A_DEV).astype(jnp.int32), A_DEV, 0).astype(jnp.float32)
        d_block = jnp.take(block_rows, beta_source, axis=2) * signs_beta
        e_block = jnp.einsum('kp,acpb->kacb', int_mat, d_block)
        e_block = lax.optimization_barrier(e_block.astype(jnp.bfloat16)).astype(jnp.float32)
        slot_table = alpha_slots[block_id]
        source_ids = slot_table[:, 0]
        pair_ids = slot_table[:, 1]
        target_ids = slot_table[:, 2]
        sign_vals = slot_table[:, 3].astype(jnp.float32)
        picked = e_block[pair_ids, source_ids] * sign_vals[:, :, None, None]
        one_hot = (target_ids[:, :, None] == strings).astype(jnp.float32)
        contrib = jnp.einsum('dqa,dqcb->dacb', one_hot, picked)
        return carry + contrib.reshape(ABLOCKS * A_DEV, 2, NB), None

    start = jnp.zeros((ABLOCKS * A_DEV, 2, NB), jnp.float32)
    sigma, unused = lax.scan(one_block, start, jnp.arange(ABLOCKS, dtype=jnp.int32))
    return sigma
```

```python
import functools

import jax
import jax.numpy as jnp
from jax import lax
from jax.experimental import pallas as pl
from jax.experimental.pallas import tpu as pltpu
from jax.sharding import PartitionSpec as P

MESH = pl.DeviceIdType.MESH
LANES = 128
F32 = jnp.float32
BF16 = jnp.bfloat16


def kernel(
    n_alpha, n_beta, cols, strings,
    coeffs_ref, ints_ref, source_ref, sign_ref, slots_ref, out_ref,
    table, wide, dvec, counts, blocks, sent, got,
    c_send, c_recv, b_send, b_recv,
):
    ia = lax.axis_index("alpha")
    ib = lax.axis_index("beta")
    pairs = ints_ref.shape[0]
    rows = 2 * strings

    barrier = pltpu.get_barrier_semaphore()
    for r in range(1, n_beta):
        pl.semaphore_signal(barrier, inc=1, device_id={"beta": lax.rem(ib + r, n_beta)}, device_id_type=MESH)
    for r in range(1, n_alpha):
        pl.semaphore_signal(barrier, inc=1, device_id={"alpha": lax.rem(ia + r, n_alpha)}, device_id_type=MESH)

    def count(j, carry):
        cap = slots_ref.shape[-1]
        pair_iota = lax.broadcasted_iota(jnp.int32, (pairs, cap), 0)
        code_iota = lax.broadcasted_iota(jnp.int32, (strings * strings, cap), 0)
        parts = []
        for half in range(2):
            entry = slots_ref[0, 2 * j + half]
            code = entry[0:1] * strings + entry[2:3]
            sign = entry[3:4].astype(F32)
            hot = jnp.where(pair_iota == entry[1:2], 1.0, 0.0).astype(BF16)
            coded = jnp.where(code_iota == code, sign, 0.0).astype(BF16)
            parts.append(lax.dot_general(coded, hot, (((1,), (1,)), ((), ())), preferred_element_type=F32))
        for a in range(strings):
            both = jnp.concatenate([part[a * strings:(a + 1) * strings] for part in parts], axis=0)
            counts[a, pl.ds(pl.multiple_of(j * rows, rows), rows), :] = both.astype(BF16)
        return carry

    first = n_alpha // 4
    lax.fori_loop(0, first, count, 0)
    pl.semaphore_wait(barrier, n_alpha + n_beta - 2)

    copies = []
    for r in range(1, n_beta):
        copy = pltpu.make_async_remote_copy(
            src_ref=coeffs_ref, dst_ref=table.at[r], send_sem=c_send.at[r], recv_sem=c_recv.at[r],
            device_id={"beta": lax.rem(ib + r, n_beta)}, device_id_type=MESH)
        copy.start()
        copies.append(copy)
    lax.fori_loop(first, n_alpha // 2, count, 0)
    for copy in copies:
        copy.wait()

    for r in range(n_beta):
        block = (coeffs_ref[...] if r == 0 else table[r]).astype(F32)
        for x in range(rows):
            wide[r, x] = jnp.broadcast_to(block[x:x + 1], (8, LANES))

    def take(src, sgn):
        lane = src & (cols - 1)
        step = lax.shift_right_logical(src, (cols - 1).bit_length())
        slot = (ib + n_beta - step) & (n_beta - 1)
        sgn = sgn.astype(F32)
        for x in range(rows):
            halves = []
            for h in (0, 8):
                index = lane[h:h + 8]
                which = slot[h:h + 8]
                value = jnp.take_along_axis(wide[0, x], index, axis=1)
                for r in range(1, n_beta):
                    value = jnp.where(which == r, jnp.take_along_axis(wide[r, x], index, axis=1), value)
                halves.append(value * sgn[h:h + 8])
            yield x, jnp.concatenate(halves, axis=0).astype(BF16)

    def gather(i, carry):
        start = pl.multiple_of(i * 16, 16)
        for x, value in take(source_ref[pl.ds(start, 16), :], sign_ref[pl.ds(start, 16), :]):
            dvec[pl.ds(start, 16), x * LANES:(x + 1) * LANES] = value
        return carry

    full = pairs // 16
    lax.fori_loop(0, full, gather, 0)
    rest = pairs - full * 16
    if rest:
        fill = jnp.zeros((16 - rest, LANES), jnp.int32)
        src = jnp.concatenate([source_ref[full * 16:pairs, :], fill], axis=0)
        sgn = jnp.concatenate([sign_ref[full * 16:pairs, :], fill], axis=0)
        for x, value in take(src, sgn):
            dvec[full * 16:full * 16 + 16, x * LANES:(x + 1) * LANES] = value

    partial = None
    for a in range(strings):
        evec = jnp.dot(ints_ref[...], dvec[0:pairs, 2 * a * LANES:2 * (a + 1) * LANES], preferred_element_type=F32)
        term = jnp.dot(counts[a], evec.astype(BF16), preferred_element_type=F32)
        partial = term if partial is None else partial + term
    for d in range(n_alpha):
        own = partial[d * strings:(d + 1) * strings]
        both = jnp.concatenate([own[:, :LANES], own[:, LANES:]], axis=0)
        blocks[d] = both
        sent[d] = both.astype(BF16)

    copies = []
    for r in range(1, n_alpha):
        to = lax.rem(ia + r, n_alpha)
        copy = pltpu.make_async_remote_copy(
            src_ref=sent.at[to], dst_ref=got.at[r], send_sem=b_send.at[r], recv_sem=b_recv.at[r],
            device_id={"alpha": to}, device_id_type=MESH)
        copy.start()
        copies.append(copy)
    total = blocks[ia]
    for r, copy in enumerate(copies, 1):
        copy.wait_recv()
        total = total + got[r].astype(F32)
    out_ref[:, 0, :] = total[:strings]
    out_ref[:, 1, :] = total[strings:]
    for copy in copies:
        copy.wait_send()


def local(n_alpha, n_beta, coeffs, integrals, beta_source, beta_sign, alpha_slots):
    strings, parts, cols = coeffs.shape
    pairs = integrals.shape[0]
    rows = strings * parts
    flat = coeffs.reshape(rows, cols)
    if cols < LANES:
        pad = ((0, 0), (0, LANES - cols))
        flat, beta_source, beta_sign = (jnp.pad(v, pad) for v in (flat, beta_source, beta_sign))
    vmem = pl.BlockSpec(memory_space=pltpu.VMEM)
    dma = pltpu.SemaphoreType.DMA
    out = pl.pallas_call(
        functools.partial(kernel, n_alpha, n_beta, cols, strings),
        out_shape=jax.ShapeDtypeStruct((strings, parts, LANES), F32),
        in_specs=[vmem] * 5,
        out_specs=vmem,
        scratch_shapes=[
            pltpu.VMEM((n_beta, rows, LANES), BF16),
            pltpu.VMEM((n_beta, rows, 8, LANES), F32),
            pltpu.VMEM((-(-pairs // 16) * 16, rows * LANES), BF16),
            pltpu.VMEM((strings, n_alpha * strings, pairs), BF16),
            pltpu.VMEM((n_alpha, rows, LANES), F32),
            pltpu.VMEM((n_alpha, rows, LANES), BF16),
            pltpu.VMEM((n_alpha, rows, LANES), BF16),
            dma((n_beta,)),
            dma((n_beta,)),
            dma((n_alpha,)),
            dma((n_alpha,)),
        ],
        compiler_params=pltpu.CompilerParams(
            collective_id=0, has_side_effects=True, vmem_limit_bytes=40 * 1024 * 1024),
    )(flat, integrals, beta_source, beta_sign, alpha_slots)
    return out[:, :, :cols]


def solution(mesh):
    in_specs = (
        P("alpha", None, "beta"),
        P(),
        P(None, "beta"),
        P(None, "beta"),
        P("alpha", None, None, None),
    )
    out_specs = P("alpha", None, "beta")
    fn = functools.partial(local, mesh.shape["alpha"], mesh.shape["beta"])
    return jax.shard_map(fn, mesh=mesh, in_specs=in_specs, out_specs=out_specs, check_vma=False)
```

```python
import functools

import jax
import jax.numpy as jnp
from jax import lax
from jax.experimental import pallas as pl
from jax.experimental.pallas import tpu as pltpu
from jax.sharding import PartitionSpec as P

MESH = pl.DeviceIdType.MESH
LANES = 128
F32 = jnp.float32
BF16 = jnp.bfloat16


def kernel(
    n_alpha, n_beta, cols, strings,
    coeffs_hbm, ints_hbm, source_hbm, sign_hbm, slots_hbm, out_ref,
    ints_ref, source_ref, sign_ref, slots_ref,
    table, wide, dvec, counts, blocks, sent, got,
    c_send, c_recv, b_send, b_recv, loaded,
):
    ia = lax.axis_index("alpha")
    ib = lax.axis_index("beta")
    pairs = ints_ref.shape[0]
    rows = 2 * strings

    loads = [
        pltpu.make_async_copy(src, dst, loaded.at[i])
        for i, (src, dst) in enumerate((
            (slots_hbm, slots_ref), (coeffs_hbm, table.at[0]), (source_hbm, source_ref),
            (sign_hbm, sign_ref), (ints_hbm, ints_ref)))
    ]
    for load in loads:
        load.start()

    barrier = pltpu.get_barrier_semaphore()
    for r in range(1, n_beta):
        pl.semaphore_signal(barrier, inc=1, device_id={"beta": lax.rem(ib + r, n_beta)}, device_id_type=MESH)
    for r in range(1, n_alpha):
        pl.semaphore_signal(barrier, inc=1, device_id={"alpha": lax.rem(ia + r, n_alpha)}, device_id_type=MESH)

    def count(j, carry):
        cap = slots_ref.shape[-1]
        pair_iota = lax.broadcasted_iota(jnp.int32, (pairs, cap), 0)
        code_iota = lax.broadcasted_iota(jnp.int32, (strings * strings, cap), 0)
        parts = []
        for half in range(2):
            entry = slots_ref[0, 2 * j + half]
            code = entry[0:1] * strings + entry[2:3]
            sign = entry[3:4].astype(F32)
            hot = jnp.where(pair_iota == entry[1:2], 1.0, 0.0).astype(BF16)
            coded = jnp.where(code_iota == code, sign, 0.0).astype(BF16)
            parts.append(lax.dot_general(coded, hot, (((1,), (1,)), ((), ())), preferred_element_type=F32))
        for a in range(strings):
            both = jnp.concatenate([part[a * strings:(a + 1) * strings] for part in parts], axis=0)
            counts[a, pl.ds(pl.multiple_of(j * rows, rows), rows), :] = both.astype(BF16)
        return carry

    loads[0].wait()
    first = n_alpha // 4
    lax.fori_loop(0, first, count, 0, unroll=4)
    pl.semaphore_wait(barrier, n_alpha + n_beta - 2)

    copies = []
    for r in range(1, n_beta):
        copy = pltpu.make_async_remote_copy(
            src_ref=coeffs_hbm, dst_ref=table.at[r], send_sem=c_send.at[r], recv_sem=c_recv.at[r],
            device_id={"beta": lax.rem(ib + r, n_beta)}, device_id_type=MESH)
        copy.start()
        copies.append(copy)
    lax.fori_loop(first, n_alpha // 2, count, 0, unroll=4)
    for load in loads[1:]:
        load.wait()
    for copy in copies:
        copy.wait()

    for r in range(n_beta):
        block = table[r].astype(F32)
        for x in range(rows):
            wide[r, x] = jnp.broadcast_to(block[x:x + 1], (8, LANES))

    def take(src, sgn):
        lane = src & (cols - 1)
        step = lax.shift_right_logical(src, (cols - 1).bit_length())
        slot = (ib + n_beta - step) & (n_beta - 1)
        sgn = sgn.astype(F32)
        for x in range(rows):
            halves = []
            for h in (0, 8):
                index = lane[h:h + 8]
                which = slot[h:h + 8]
                value = jnp.take_along_axis(wide[0, x], index, axis=1)
                for r in range(1, n_beta):
                    value = jnp.where(which == r, jnp.take_along_axis(wide[r, x], index, axis=1), value)
                halves.append(value * sgn[h:h + 8])
            yield x, jnp.concatenate(halves, axis=0).astype(BF16)

    def gather(i, carry):
        start = pl.multiple_of(i * 16, 16)
        for x, value in take(source_ref[pl.ds(start, 16), :], sign_ref[pl.ds(start, 16), :]):
            dvec[pl.ds(start, 16), x * LANES:(x + 1) * LANES] = value
        return carry

    full = pairs // 16
    lax.fori_loop(0, full, gather, 0, unroll=2)
    rest = pairs - full * 16
    if rest:
        fill = jnp.zeros((16 - rest, LANES), jnp.int32)
        src = jnp.concatenate([source_ref[full * 16:pairs, :], fill], axis=0)
        sgn = jnp.concatenate([sign_ref[full * 16:pairs, :], fill], axis=0)
        for x, value in take(src, sgn):
            dvec[full * 16:full * 16 + 16, x * LANES:(x + 1) * LANES] = value

    partial = None
    for a in range(strings):
        evec = jnp.dot(ints_ref[...], dvec[0:pairs, 2 * a * LANES:2 * (a + 1) * LANES], preferred_element_type=F32)
        term = jnp.dot(counts[a], evec.astype(BF16), preferred_element_type=F32)
        partial = term if partial is None else partial + term
    for d in range(n_alpha):
        own = partial[d * strings:(d + 1) * strings]
        both = jnp.concatenate([own[:, :LANES], own[:, LANES:]], axis=0)
        blocks[d] = both
        sent[d] = both.astype(BF16)

    copies = []
    for r in range(1, n_alpha):
        to = lax.rem(ia + r, n_alpha)
        copy = pltpu.make_async_remote_copy(
            src_ref=sent.at[to], dst_ref=got.at[r], send_sem=b_send.at[r], recv_sem=b_recv.at[r],
            device_id={"alpha": to}, device_id_type=MESH)
        copy.start()
        copies.append(copy)
    total = blocks[ia]
    for r, copy in enumerate(copies, 1):
        copy.wait_recv()
        total = total + got[r].astype(F32)
    out_ref[:, 0, :] = total[:strings]
    out_ref[:, 1, :] = total[strings:]
    for copy in copies:
        copy.wait_send()


def local(n_alpha, n_beta, coeffs, integrals, beta_source, beta_sign, alpha_slots):
    strings, parts, cols = coeffs.shape
    pairs = integrals.shape[0]
    rows = strings * parts
    flat = coeffs.reshape(rows, cols)
    if cols < LANES:
        pad = ((0, 0), (0, LANES - cols))
        flat, beta_source, beta_sign = (jnp.pad(v, pad) for v in (flat, beta_source, beta_sign))
    vmem = pl.BlockSpec(memory_space=pltpu.VMEM)
    dma = pltpu.SemaphoreType.DMA
    out = pl.pallas_call(
        functools.partial(kernel, n_alpha, n_beta, cols, strings),
        out_shape=jax.ShapeDtypeStruct((strings, parts, LANES), F32),
        in_specs=[pl.BlockSpec(memory_space=pltpu.HBM)] * 5,
        out_specs=vmem,
        scratch_shapes=[
            pltpu.VMEM(integrals.shape, BF16),
            pltpu.VMEM(beta_source.shape, jnp.int32),
            pltpu.VMEM(beta_sign.shape, jnp.int32),
            pltpu.VMEM(alpha_slots.shape, jnp.int32),
            pltpu.VMEM((n_beta, rows, LANES), BF16),
            pltpu.VMEM((n_beta, rows, 8, LANES), F32),
            pltpu.VMEM((-(-pairs // 16) * 16, rows * LANES), BF16),
            pltpu.VMEM((strings, n_alpha * strings, pairs), BF16),
            pltpu.VMEM((n_alpha, rows, LANES), F32),
            pltpu.VMEM((n_alpha, rows, LANES), BF16),
            pltpu.VMEM((n_alpha, rows, LANES), BF16),
            dma((n_beta,)),
            dma((n_beta,)),
            dma((n_alpha,)),
            dma((n_alpha,)),
            dma((5,)),
        ],
        compiler_params=pltpu.CompilerParams(
            collective_id=0, has_side_effects=True, vmem_limit_bytes=40 * 1024 * 1024),
    )(flat, integrals, beta_source, beta_sign, alpha_slots)
    return out[:, :, :cols]


def solution(mesh):
    in_specs = (
        P("alpha", None, "beta"),
        P(),
        P(None, "beta"),
        P(None, "beta"),
        P("alpha", None, None, None),
    )
    out_specs = P("alpha", None, "beta")
    fn = functools.partial(local, mesh.shape["alpha"], mesh.shape["beta"])
    return jax.shard_map(fn, mesh=mesh, in_specs=in_specs, out_specs=out_specs, check_vma=False)
```

```python
import functools

import jax
import jax.numpy as jnp
from jax import lax
from jax.experimental import pallas as pl
from jax.experimental.pallas import tpu as pltpu
from jax.sharding import PartitionSpec as P

MESH = pl.DeviceIdType.MESH
LANES = 128
F32 = jnp.float32
BF16 = jnp.bfloat16


def kernel(
    n_alpha, n_beta, cols, strings,
    coeffs_hbm, ints_hbm, source_hbm, sign_hbm, slots_hbm, out_ref,
    ints_ref, source_ref, sign_ref, slots_ref,
    table, wide, dvec, counts, blocks, sent, got,
    c_send, c_recv, b_send, b_recv, loaded,
):
    ia = lax.axis_index("alpha")
    ib = lax.axis_index("beta")
    pairs = ints_ref.shape[0]
    rows = 2 * strings

    loads = [
        pltpu.make_async_copy(src, dst, loaded.at[i])
        for i, (src, dst) in enumerate((
            (slots_hbm, slots_ref), (coeffs_hbm, table.at[0]), (source_hbm, source_ref),
            (sign_hbm, sign_ref), (ints_hbm, ints_ref)))
    ]
    for load in loads:
        load.start()

    barrier = pltpu.get_barrier_semaphore()
    for r in range(1, n_beta):
        pl.semaphore_signal(barrier, inc=1, device_id={"beta": lax.rem(ib + r, n_beta)}, device_id_type=MESH)
    for r in range(1, n_alpha):
        pl.semaphore_signal(barrier, inc=1, device_id={"alpha": lax.rem(ia + r, n_alpha)}, device_id_type=MESH)

    def count(j, carry):
        cap = slots_ref.shape[-1]
        pair_iota = lax.broadcasted_iota(jnp.int32, (pairs, cap), 0)
        code_iota = lax.broadcasted_iota(jnp.int32, (strings * strings, cap), 0)
        parts = []
        for half in range(2):
            entry = slots_ref[0, 2 * j + half]
            code = entry[0:1] * strings + entry[2:3]
            sign = entry[3:4].astype(F32)
            hot = jnp.where(pair_iota == entry[1:2], 1.0, 0.0).astype(BF16)
            coded = jnp.where(code_iota == code, sign, 0.0).astype(BF16)
            parts.append(lax.dot_general(coded, hot, (((1,), (1,)), ((), ())), preferred_element_type=F32))
        for a in range(strings):
            both = jnp.concatenate([part[a * strings:(a + 1) * strings] for part in parts], axis=0)
            counts[a, pl.ds(pl.multiple_of(j * rows, rows), rows), :] = both.astype(BF16)
        return carry

    loads[0].wait()
    first = n_alpha // 4
    lax.fori_loop(0, first, count, 0, unroll=4)
    pl.semaphore_wait(barrier, n_alpha + n_beta - 2)

    copies = []
    for r in range(1, n_beta):
        copy = pltpu.make_async_remote_copy(
            src_ref=coeffs_hbm, dst_ref=table.at[r], send_sem=c_send.at[r], recv_sem=c_recv.at[r],
            device_id={"beta": lax.rem(ib + r, n_beta)}, device_id_type=MESH)
        copy.start()
        copies.append(copy)
    lax.fori_loop(first, n_alpha // 2, count, 0, unroll=4)
    for load in loads[1:]:
        load.wait()
    for copy in copies:
        copy.wait()

    for r in range(n_beta):
        block = table[r].astype(F32)
        for x in range(rows):
            wide[r, x] = jnp.broadcast_to(block[x:x + 1], (8, LANES))

    def take(src, sgn):
        lane = src & (cols - 1)
        step = lax.shift_right_logical(src, (cols - 1).bit_length())
        slot = (ib + n_beta - step) & (n_beta - 1)
        sgn = sgn.astype(F32)
        for x in range(rows):
            halves = []
            for h in (0, 8):
                index = lane[h:h + 8]
                which = slot[h:h + 8]
                value = jnp.take_along_axis(wide[0, x], index, axis=1)
                for r in range(1, n_beta):
                    value = jnp.where(which == r, jnp.take_along_axis(wide[r, x], index, axis=1), value)
                halves.append(value * sgn[h:h + 8])
            yield x, jnp.concatenate(halves, axis=0).astype(BF16)

    def gather(i, carry):
        start = pl.multiple_of(i * 16, 16)
        for x, value in take(source_ref[pl.ds(start, 16), :], sign_ref[pl.ds(start, 16), :]):
            dvec[pl.ds(start, 16), x * LANES:(x + 1) * LANES] = value
        return carry

    full = pairs // 16
    lax.fori_loop(0, full, gather, 0, unroll=2)
    rest = pairs - full * 16
    if rest:
        fill = jnp.zeros((16 - rest, LANES), jnp.int32)
        src = jnp.concatenate([source_ref[full * 16:pairs, :], fill], axis=0)
        sgn = jnp.concatenate([sign_ref[full * 16:pairs, :], fill], axis=0)
        for x, value in take(src, sgn):
            dvec[full * 16:full * 16 + 16, x * LANES:(x + 1) * LANES] = value

    partial = None
    for a in range(strings):
        evec = jnp.dot(ints_ref[...], dvec[0:pairs, 2 * a * LANES:2 * (a + 1) * LANES], preferred_element_type=F32)
        term = jnp.dot(counts[a], evec.astype(BF16), preferred_element_type=F32)
        partial = term if partial is None else partial + term
    for d in range(n_alpha):
        own = partial[d * strings:(d + 1) * strings]
        both = jnp.concatenate([own[:, :LANES], own[:, LANES:]], axis=0)
        blocks[d] = both
        sent[d] = both.astype(BF16)

    copies = []
    for r in range(1, n_alpha):
        to = lax.rem(ia + r, n_alpha)
        copy = pltpu.make_async_remote_copy(
            src_ref=sent.at[to], dst_ref=got.at[r], send_sem=b_send.at[r], recv_sem=b_recv.at[r],
            device_id={"alpha": to}, device_id_type=MESH)
        copy.start()
        copies.append(copy)
    total = blocks[ia]
    for r, copy in enumerate(copies, 1):
        copy.wait_recv()
        total = total + got[r].astype(F32)
    out_ref[:, 0, :] = total[:strings]
    out_ref[:, 1, :] = total[strings:]
    for copy in copies:
        copy.wait_send()


def local(n_alpha, n_beta, coeffs, integrals, beta_source, beta_sign, alpha_slots):
    strings, parts, cols = coeffs.shape
    pairs = integrals.shape[0]
    rows = strings * parts
    flat = coeffs.reshape(rows, cols)
    if cols < LANES:
        pad = ((0, 0), (0, LANES - cols))
        flat, beta_source, beta_sign = (jnp.pad(v, pad) for v in (flat, beta_source, beta_sign))
    vmem = pl.BlockSpec(memory_space=pltpu.VMEM)
    dma = pltpu.SemaphoreType.DMA
    out = pl.pallas_call(
        functools.partial(kernel, n_alpha, n_beta, cols, strings),
        out_shape=jax.ShapeDtypeStruct((strings, parts, LANES), F32),
        in_specs=[pl.BlockSpec(memory_space=pltpu.HBM)] * 5,
        out_specs=vmem,
        scratch_shapes=[
            pltpu.VMEM(integrals.shape, BF16),
            pltpu.VMEM(beta_source.shape, jnp.int32),
            pltpu.VMEM(beta_sign.shape, jnp.int32),
            pltpu.VMEM(alpha_slots.shape, jnp.int32),
            pltpu.VMEM((n_beta, rows, LANES), BF16),
            pltpu.VMEM((n_beta, rows, 8, LANES), F32),
            pltpu.VMEM((-(-pairs // 16) * 16, rows * LANES), BF16),
            pltpu.VMEM((strings, n_alpha * strings, pairs), BF16),
            pltpu.VMEM((n_alpha, rows, LANES), F32),
            pltpu.VMEM((n_alpha, rows, LANES), BF16),
            pltpu.VMEM((n_alpha, rows, LANES), BF16),
            dma((n_beta,)),
            dma((n_beta,)),
            dma((n_alpha,)),
            dma((n_alpha,)),
            dma((5,)),
        ],
        compiler_params=pltpu.CompilerParams(
            collective_id=0, has_side_effects=True, vmem_limit_bytes=63 * 1024 * 1024),
    )(flat, integrals, beta_source, beta_sign, alpha_slots)
    return out[:, :, :cols]


def solution(mesh):
    in_specs = (
        P("alpha", None, "beta"),
        P(),
        P(None, "beta"),
        P(None, "beta"),
        P("alpha", None, None, None),
    )
    out_specs = P("alpha", None, "beta")
    fn = functools.partial(local, mesh.shape["alpha"], mesh.shape["beta"])
    return jax.shard_map(fn, mesh=mesh, in_specs=in_specs, out_specs=out_specs, check_vma=False)
```

```python
import functools

import jax
import jax.numpy as jnp
from jax import lax
from jax.experimental import pallas as pl
from jax.experimental.pallas import tpu as pltpu
from jax.sharding import PartitionSpec as P

MESH = pl.DeviceIdType.MESH
LANES = 128
F32 = jnp.float32
BF16 = jnp.bfloat16


def kernel(
    n_alpha, n_beta, cols, strings,
    coeffs_hbm, ints_hbm, source_hbm, sign_hbm, slots_hbm, out_ref,
    ints_ref, source_ref, sign_ref, slots_ref,
    table, wide, dvec, counts, blocks, sent, got,
    c_send, c_recv, b_send, b_recv, loaded,
):
    ia = lax.axis_index("alpha")
    ib = lax.axis_index("beta")
    pairs = ints_ref.shape[0]
    rows = 2 * strings

    loads = [
        pltpu.make_async_copy(src, dst, loaded.at[i])
        for i, (src, dst) in enumerate((
            (slots_hbm, slots_ref), (coeffs_hbm, table.at[0]), (source_hbm, source_ref),
            (sign_hbm, sign_ref), (ints_hbm, ints_ref)))
    ]
    for load in loads:
        load.start()

    barrier = pltpu.get_barrier_semaphore()
    for r in range(1, n_beta):
        pl.semaphore_signal(barrier, inc=1, device_id={"beta": lax.rem(ib + r, n_beta)}, device_id_type=MESH)
    for r in range(1, n_alpha):
        pl.semaphore_signal(barrier, inc=1, device_id={"alpha": lax.rem(ia + r, n_alpha)}, device_id_type=MESH)

    def count(j, carry):
        cap = slots_ref.shape[-1]
        pair_iota = lax.broadcasted_iota(jnp.int32, (pairs, cap), 0)
        code_iota = lax.broadcasted_iota(jnp.int32, (strings * strings, cap), 0)
        parts = []
        for half in range(2):
            entry = slots_ref[0, 2 * j + half]
            code = entry[0:1] * strings + entry[2:3]
            sign = entry[3:4].astype(F32)
            hot = jnp.where(pair_iota == entry[1:2], 1.0, 0.0).astype(BF16)
            coded = jnp.where(code_iota == code, sign, 0.0).astype(BF16)
            parts.append(lax.dot_general(coded, hot, (((1,), (1,)), ((), ())), preferred_element_type=F32))
        for a in range(strings):
            both = jnp.concatenate([part[a * strings:(a + 1) * strings] for part in parts], axis=0)
            counts[a, pl.ds(pl.multiple_of(j * rows, rows), rows), :] = both.astype(BF16)
        return carry

    loads[0].wait()
    first = n_alpha // 4
    lax.fori_loop(0, first, count, 0, unroll=4)
    pl.semaphore_wait(barrier, n_alpha + n_beta - 2)

    copies = []
    for r in range(1, n_beta):
        copy = pltpu.make_async_remote_copy(
            src_ref=coeffs_hbm, dst_ref=table.at[r], send_sem=c_send.at[r], recv_sem=c_recv.at[r],
            device_id={"beta": lax.rem(ib + r, n_beta)}, device_id_type=MESH)
        copy.start()
        copies.append(copy)
    lax.fori_loop(first, n_alpha // 2, count, 0, unroll=4)
    for load in loads[1:]:
        load.wait()
    for copy in copies:
        copy.wait()

    for r in range(n_beta):
        block = table[r].astype(F32)
        for x in range(rows):
            wide[r, x] = jnp.broadcast_to(block[x:x + 1], (8, LANES))

    def take(src, sgn, span=range(rows)):
        lane = src & (cols - 1)
        step = lax.shift_right_logical(src, (cols - 1).bit_length())
        slot = (ib + n_beta - step) & (n_beta - 1)
        sgn = sgn.astype(F32)
        for x in span:
            halves = []
            for h in (0, 8):
                index = lane[h:h + 8]
                which = slot[h:h + 8]
                value = jnp.take_along_axis(wide[0, x], index, axis=1)
                for r in range(1, n_beta):
                    value = jnp.where(which == r, jnp.take_along_axis(wide[r, x], index, axis=1), value)
                halves.append(value * sgn[h:h + 8])
            yield x, jnp.concatenate(halves, axis=0).astype(BF16)

    def gather(i, carry):
        start = pl.multiple_of(i * 16, 16)
        for x, value in take(source_ref[pl.ds(start, 16), :], sign_ref[pl.ds(start, 16), :]):
            dvec[pl.ds(start, 16), x * LANES:(x + 1) * LANES] = value
        return carry

    full = pairs // 16
    rest = pairs - full * 16
    inline = n_beta <= 2
    if not inline:
        lax.fori_loop(0, full, gather, 0, unroll=2)

    def tile(i, span):
        if i < full:
            src, sgn = source_ref[i * 16:i * 16 + 16, :], sign_ref[i * 16:i * 16 + 16, :]
        else:
            fill = jnp.zeros((16 - rest, LANES), jnp.int32)
            src = jnp.concatenate([source_ref[full * 16:pairs, :], fill], axis=0)
            sgn = jnp.concatenate([sign_ref[full * 16:pairs, :], fill], axis=0)
        for x, value in take(src, sgn, span):
            dvec[i * 16:i * 16 + 16, x * LANES:(x + 1) * LANES] = value

    if rest and not inline:
        tile(full, range(rows))

    partial = None
    for a in range(strings):
        if inline:
            for i in range(-(-pairs // 16)):
                tile(i, range(2 * a, 2 * a + 2))
        evec = jnp.dot(ints_ref[...], dvec[0:pairs, 2 * a * LANES:2 * (a + 1) * LANES], preferred_element_type=F32)
        term = jnp.dot(counts[a], evec.astype(BF16), preferred_element_type=F32)
        partial = term if partial is None else partial + term
    for d in range(n_alpha):
        own = partial[d * strings:(d + 1) * strings]
        both = jnp.concatenate([own[:, :LANES], own[:, LANES:]], axis=0)
        blocks[d] = both
        sent[d] = both.astype(BF16)

    copies = []
    for r in range(1, n_alpha):
        to = lax.rem(ia + r, n_alpha)
        copy = pltpu.make_async_remote_copy(
            src_ref=sent.at[to], dst_ref=got.at[r], send_sem=b_send.at[r], recv_sem=b_recv.at[r],
            device_id={"alpha": to}, device_id_type=MESH)
        copy.start()
        copies.append(copy)
    total = blocks[ia]
    for r, copy in enumerate(copies, 1):
        copy.wait_recv()
        total = total + got[r].astype(F32)
    out_ref[:, 0, :] = total[:strings]
    out_ref[:, 1, :] = total[strings:]
    for copy in copies:
        copy.wait_send()


def local(n_alpha, n_beta, coeffs, integrals, beta_source, beta_sign, alpha_slots):
    strings, parts, cols = coeffs.shape
    pairs = integrals.shape[0]
    rows = strings * parts
    flat = coeffs.reshape(rows, cols)
    if cols < LANES:
        pad = ((0, 0), (0, LANES - cols))
        flat, beta_source, beta_sign = (jnp.pad(v, pad) for v in (flat, beta_source, beta_sign))
    vmem = pl.BlockSpec(memory_space=pltpu.VMEM)
    dma = pltpu.SemaphoreType.DMA
    out = pl.pallas_call(
        functools.partial(kernel, n_alpha, n_beta, cols, strings),
        out_shape=jax.ShapeDtypeStruct((strings, parts, LANES), F32),
        in_specs=[pl.BlockSpec(memory_space=pltpu.HBM)] * 5,
        out_specs=vmem,
        scratch_shapes=[
            pltpu.VMEM(integrals.shape, BF16),
            pltpu.VMEM(beta_source.shape, jnp.int32),
            pltpu.VMEM(beta_sign.shape, jnp.int32),
            pltpu.VMEM(alpha_slots.shape, jnp.int32),
            pltpu.VMEM((n_beta, rows, LANES), BF16),
            pltpu.VMEM((n_beta, rows, 8, LANES), F32),
            pltpu.VMEM((-(-pairs // 16) * 16, rows * LANES), BF16),
            pltpu.VMEM((strings, n_alpha * strings, pairs), BF16),
            pltpu.VMEM((n_alpha, rows, LANES), F32),
            pltpu.VMEM((n_alpha, rows, LANES), BF16),
            pltpu.VMEM((n_alpha, rows, LANES), BF16),
            dma((n_beta,)),
            dma((n_beta,)),
            dma((n_alpha,)),
            dma((n_alpha,)),
            dma((5,)),
        ],
        compiler_params=pltpu.CompilerParams(
            collective_id=0, has_side_effects=True, vmem_limit_bytes=63 * 1024 * 1024),
    )(flat, integrals, beta_source, beta_sign, alpha_slots)
    return out[:, :, :cols]


def solution(mesh):
    in_specs = (
        P("alpha", None, "beta"),
        P(),
        P(None, "beta"),
        P(None, "beta"),
        P("alpha", None, None, None),
    )
    out_specs = P("alpha", None, "beta")
    fn = functools.partial(local, mesh.shape["alpha"], mesh.shape["beta"])
    return jax.shard_map(fn, mesh=mesh, in_specs=in_specs, out_specs=out_specs, check_vma=False)
```
